32 devices in a mesh: ctx: 16 (over z, y, core), tp: 2 (over x).
Axes of the slice: x: 2, y: 2, z: 4, core: 2. Of those that a mesh axis runs over, the one named last changes fastest.
Arguments:
- queries: bfloat16 [4096, 4096], P('ctx', 'tp'), may hold values from -112 to 112
- keys: bfloat16 [4096, 1024], P('ctx', 'tp'), may hold values from -4.5 to 4.5
- values: bfloat16 [4096, 1024], P('ctx', 'tp'), may hold values from -6 to 6
- head_kind: int32 [8], replicated, may hold values from 0 to 1, as said below
- sink_len: int32 [8], replicated, may hold values from 32 to 128, as said below
- window_len: int32 [8], replicated, may hold values from 512 to 1024, as said below
- w_out: bfloat16 [4096, 4096], P('tp'), may hold values from -0.375 to 0.375
Outputs:
- mixed: bfloat16 [4096, 4096], P(('ctx', 'tp'))
The draws below stay inside these ranges and needn't reach their ends.
Inputs may be any that keep to these rules, and one draw needn't show every extreme that they name: `head_kind`: exactly 4 entries are 1. `sink_len`: some head with head_kind 0 has exactly 128. `window_len`: some head with head_kind 0 has exactly 1024.
All inputs are finite; a program needn't handle non-finite values.
Results may differ from the reference program's by a relative error of at most 0.014.
Values may be sent and summed in bfloat16 or wider, within the bound.
A program may use at most 128 MiB of HBM per device.

```python
import math
import jax
import jax.numpy as jnp
from jax import lax

H = 32
KVH = 8
HD = 128
D = 4096
GROUP = 4
TOKENS = 4096
SINK = 128
WINDOW = 1024


def query_key_pair(key):
    query_noise = jax.random.normal(jax.random.fold_in(key, 101), (TOKENS, KVH, GROUP, HD), jnp.float32)
    key_noise = jax.random.normal(jax.random.fold_in(key, 102), (TOKENS, KVH, HD), jnp.float32)
    query_draw = jnp.clip(2.0 * query_noise, -8.0, 8.0)
    key_draw = jnp.clip(key_noise, -4.0, 4.0)
    return (query_draw.reshape(TOKENS, H * HD), key_draw.reshape(TOKENS, KVH * HD))


def draw_queries(key, part):
    return query_key_pair(key)[0].astype(jnp.bfloat16)


def draw_keys(key, part):
    return query_key_pair(key)[1].astype(jnp.bfloat16)


def head_table(key):
    order = jax.random.permutation(jax.random.fold_in(key, 201), KVH)
    kinds = (order < KVH // 2).astype(jnp.int32)
    widest = order == KVH // 2
    sinks = jax.random.randint(jax.random.fold_in(key, 202), (KVH,), SINK // 4, SINK + 1)
    windows = jax.random.randint(jax.random.fold_in(key, 203), (KVH,), WINDOW // 2, WINDOW + 1)
    sinks = jnp.where(widest, SINK, sinks).astype(jnp.int32)
    windows = jnp.where(widest, WINDOW, windows).astype(jnp.int32)
    return (kinds, sinks, windows)


def draw_head_kind(key, part):
    return head_table(key)[0]


def draw_sink_len(key, part):
    return head_table(key)[1]


def draw_window_len(key, part):
    return head_table(key)[2]


def block_levels(rng, shape, shards, least, high):
    def one(dim, parts):
        heights = jax.random.uniform(jax.random.fold_in(jax.random.fold_in(rng, 6), dim), (parts,), jnp.float32, least / len(shards), high / len(shards))
        return jnp.repeat(jnp.exp(heights), shape[dim] // parts).reshape((-1,) + (1,) * (len(shape) - dim - 1))

    loudness = one(*shards[0])
    for cut in shards[1:]:
        loudness = loudness * one(*cut)
    return loudness


def centred(stream_key, extent, deviation, bound, split=(), kind=jnp.bfloat16):
    result = deviation * jax.random.normal(stream_key, extent, jnp.float32)
    if split:
        result = result * block_levels(stream_key, extent, split, -0.22, 0.18)
    return jnp.clip(result, -bound, bound).astype(kind)


def setup_inputs(seed: int = 0) -> dict:
    splits = jax.random.split(jax.random.key(seed), 8)
    return {
        "queries": draw_queries(jax.random.fold_in(splits[7], 71), 0),
        "keys": draw_keys(jax.random.fold_in(splits[7], 71), 0),
        "values": centred(splits[2], (TOKENS, KVH * HD), 1.0, 6.0, ((0, 16), (1, 2))),
        "head_kind": draw_head_kind(jax.random.fold_in(splits[7], 71), 0),
        "sink_len": draw_sink_len(jax.random.fold_in(splits[7], 71), 0),
        "window_len": draw_window_len(jax.random.fold_in(splits[7], 71), 0),
        "w_out": centred(splits[6], (H * HD, D), (H * HD // 16) ** -0.5, 0.375, ((0, 2),)),
    }


def reference(queries, keys, values, head_kind, sink_len, window_len, w_out):
    score_scale = 1.0 / math.sqrt(HD)
    q_all = queries.reshape(TOKENS, KVH, GROUP, HD)
    k_all = keys.reshape(TOKENS, KVH, HD)
    v_all = values.reshape(TOKENS, KVH, HD)
    positions = jnp.arange(TOKENS, dtype=jnp.int32)
    block_size = min(512, TOKENS)

    def head_output(kv_head):
        q_head = lax.dynamic_index_in_dim(q_all, kv_head, 1, keepdims=False).astype(jnp.float32)
        k_head = lax.dynamic_index_in_dim(k_all, kv_head, 1, keepdims=False).astype(jnp.float32)
        v_head = lax.dynamic_index_in_dim(v_all, kv_head, 1, keepdims=False).astype(jnp.float32)
        retrieval = head_kind[kv_head] == 1
        sink_count = sink_len[kv_head]
        window = window_len[kv_head]

        def block_output(block_index):
            q_block = lax.dynamic_slice_in_dim(q_head, block_index * block_size, block_size, 0)
            q_pos = block_index * block_size + jnp.arange(block_size, dtype=jnp.int32)
            scores = jnp.einsum('igd,jd->igj', q_block, k_head) * score_scale
            before = positions[None, :] <= q_pos[:, None]
            in_window = positions[None, :] > q_pos[:, None] - window
            in_sink = positions[None, :] < sink_count
            allowed = (before & (retrieval | in_window | in_sink))[:, None, :]
            top_score = lax.optimization_barrier(jnp.max(jnp.where(allowed, scores, -jnp.inf), axis=2, keepdims=True))
            weights = jnp.where(allowed, jnp.exp(scores - top_score), 0.0)
            weight_sum = lax.optimization_barrier(jnp.sum(weights, axis=2))
            rounded = lax.optimization_barrier(weights.astype(jnp.bfloat16)).astype(jnp.float32)
            blended = jnp.einsum('igj,jd->igd', rounded, v_head) / weight_sum[:, :, None]
            return blended.astype(jnp.bfloat16)
        blocks_out = lax.map(block_output, jnp.arange(TOKENS // block_size, dtype=jnp.int32))
        return blocks_out.reshape(TOKENS, GROUP * HD)
    per_head = lax.map(head_output, jnp.arange(KVH, dtype=jnp.int32))
    attention = jnp.transpose(per_head, (1, 0, 2)).reshape(TOKENS, KVH * GROUP * HD)
    return jnp.dot(attention, w_out, preferred_element_type=jnp.float32).astype(jnp.bfloat16)
```

```python
import functools
import math

import jax
import jax.numpy as jnp
from jax import lax
from jax.experimental import pallas as pl
from jax.experimental.pallas import tpu as pltpu
from jax.sharding import PartitionSpec as P

HD = 128
LANES = 4
CHUNK = 512
LOW = -1e30
MESH = pl.DeviceIdType.MESH


def layer_kernel(
    ctx_count, tp_count, kind_ref, sink_ref, window_ref, q_ref, k_ref, v_ref, w_hbm, out_ref,
    kv_buf, w_buf, top_ref, acc_ref, bias_ref, attn_ref, part_ref, send_buf, recv_buf, own_ref,
    w_sem, block_send, block_recv, sum_send, sum_recv,
):
    rank = lax.axis_index("ctx")
    tp_rank = lax.axis_index("tp")
    rows, kv_cols = k_ref.shape
    local_kv = kv_cols // HD
    group = q_ref.shape[1] // kv_cols
    planes = ctx_count // LANES
    plane = lax.div(rank, LANES)
    lane = lax.rem(rank, LANES)
    odd = lax.rem(lane, 2)
    high = lax.div(lane, 2)
    sibling = rank + 1 - 2 * odd
    across = rank + 2 - 4 * high
    factor = math.log2(math.e) / math.sqrt(HD)
    out_cols = w_buf.shape[1]
    chunks = out_cols // CHUNK
    share = rows // tp_count

    w_copy = pltpu.make_async_copy(w_hbm, w_buf, w_sem)
    w_copy.start()

    barrier = pltpu.get_barrier_semaphore()

    def greet(where):
        pl.semaphore_signal(barrier, inc=1, device_id=where, device_id_type=MESH)

    greet({"ctx": sibling})
    greet({"ctx": across})
    for step in range(1, tp_count):
        greet({"tp": lax.rem(tp_rank + step, tp_count)})

    @pl.when(plane > 0)
    def _():
        greet({"ctx": rank - LANES})

    @pl.when(plane < planes - 1)
    def _():
        greet({"ctx": rank + LANES})

    own_rows = pl.ds(pl.multiple_of(rank * rows, rows), rows)
    kv_buf[own_rows, :kv_cols] = k_ref[...]
    kv_buf[own_rows, kv_cols:] = v_ref[...]
    top_ref[...] = jnp.full_like(top_ref, LOW)
    acc_ref[...] = jnp.zeros_like(acc_ref)

    beside_planes = jnp.minimum(plane, 1) + jnp.minimum(planes - 1 - plane, 1)
    pl.semaphore_wait(barrier, 1 + tp_count + beside_planes)

    def block_copy(block, way, target):
        where = pl.ds(pl.multiple_of(block * rows, rows), rows)
        return pltpu.make_async_remote_copy(
            src_ref=kv_buf.at[where],
            dst_ref=kv_buf.at[where],
            send_sem=block_send.at[block, way],
            recv_sem=block_recv.at[block],
            device_id={"ctx": target},
            device_id_type=MESH,
        )

    def send_on(block):
        @pl.when(plane < planes - 1)
        def _():
            block_copy(block, 0, rank + LANES).start()

        block_copy(block, 2, across).start()
        block_copy(block, 1, sibling).start()

    def fold(first_block):
        span = 2 * rows
        key_rows = pl.ds(pl.multiple_of(first_block * rows, rows), span)
        parts = span // HD

        def head_step(head, carry):
            index = tp_rank * local_kv + head
            reach = jnp.where(kind_ref[index] == 1, jnp.int32(2**30), window_ref[index])
            key_pos = first_block * rows + lax.broadcasted_iota(jnp.int32, (rows, span), 1)
            behind = key_pos - rank * rows - lax.broadcasted_iota(jnp.int32, (rows, span), 0)
            allowed = (behind <= 0) & ((behind > -reach) | (key_pos < sink_ref[index]))
            bias_ref[...] = jnp.where(allowed, 0.0, LOW)
            key_block = kv_buf[key_rows, pl.ds(pl.multiple_of(head * HD, HD), HD)]
            value_block = kv_buf[key_rows, pl.ds(pl.multiple_of(kv_cols + head * HD, HD), HD)]
            value_block = jnp.concatenate([value_block, jnp.ones_like(value_block)], axis=1)
            for member in range(group):
                slot = head * group + member
                query = q_ref[:, pl.ds(pl.multiple_of(slot * HD, HD), HD)]
                scores = lax.dot_general(
                    query, key_block, (((1,), (1,)), ((), ())),
                    preferred_element_type=jnp.float32,
                )
                scores = scores * factor + bias_ref[...]
                before = top_ref[slot]
                top = jnp.maximum(before, jnp.max(scores, axis=1, keepdims=True))
                weights = jnp.concatenate(
                    [
                        jnp.exp2(scores[:, i * HD : (i + 1) * HD] - top).astype(jnp.bfloat16)
                        for i in range(parts)
                    ],
                    axis=1,
                )
                keep = jnp.exp2(before - top)
                blended = jnp.dot(weights, value_block, preferred_element_type=jnp.float32)
                top_ref[slot] = top
                acc_ref[slot, :, :HD] = acc_ref[slot, :, :HD] * keep + blended[:, :HD]
                acc_ref[slot, :, HD:] = acc_ref[slot, :, HD:] * keep + blended[:, HD:]
            return carry

        lax.fori_loop(0, local_kv, head_step, 0)

    send_on(rank)

    def plane_step(back, carry):
        mine = rank - back * LANES
        beside = sibling - back * LANES
        far = across - back * LANES
        far_beside = far + 1 - 2 * odd
        near_pair = mine - odd
        far_pair = far - odd

        @pl.when(back < plane)
        def _():
            block_copy(mine - LANES, 0, rank).wait_recv()
            send_on(mine - LANES)

        block_copy(beside, 0, rank).wait_recv()
        fold(near_pair)
        block_copy(far, 0, rank).wait_recv()
        block_copy(far, 1, sibling).start()
        block_copy(far_beside, 0, rank).wait_recv()

        @pl.when(far_pair <= rank)
        def _():
            fold(far_pair)

        return carry

    lax.fori_loop(0, plane + 1, plane_step, 0)

    for slot in range(local_kv * group):
        attn_ref[:, slot * HD : (slot + 1) * HD] = (
            acc_ref[slot, :, :HD] / acc_ref[slot, :, HD:]
        ).astype(jnp.bfloat16)
    w_copy.wait()

    def sum_copy(target, source, chunk):
        where = pl.ds(pl.multiple_of(chunk * CHUNK, CHUNK), CHUNK)
        return pltpu.make_async_remote_copy(
            src_ref=send_buf.at[pl.ds(pl.multiple_of(target * share, share), share), where],
            dst_ref=recv_buf.at[pl.ds(pl.multiple_of(source * share, share), share), where],
            send_sem=sum_send.at[target, chunk],
            recv_sem=sum_recv.at[source, chunk],
            device_id={"tp": target},
            device_id_type=MESH,
        )

    def project(chunk, carry):
        where = pl.ds(pl.multiple_of(chunk * CHUNK, CHUNK), CHUNK)
        part_ref[...] = jnp.dot(attn_ref[...], w_buf[:, where], preferred_element_type=jnp.float32)
        send_buf[:, where] = part_ref[...].astype(jnp.bfloat16)
        for step in range(1, tp_count):
            sum_copy(lax.rem(tp_rank + step, tp_count), tp_rank, chunk).start()
        own_ref[:, where] = part_ref[pl.ds(pl.multiple_of(tp_rank * share, share), share), :]
        return carry

    lax.fori_loop(0, chunks, project, 0)

    def collect(chunk, carry):
        where = pl.ds(pl.multiple_of(chunk * CHUNK, CHUNK), CHUNK)
        total = own_ref[:, where]
        for step in range(1, tp_count):
            source = lax.rem(tp_rank + step, tp_count)
            sum_copy(source, source, chunk).wait_recv()
            rows_from = pl.ds(pl.multiple_of(source * share, share), share)
            total = total + recv_buf[rows_from, where].astype(jnp.float32)
        out_ref[:, where] = total.astype(jnp.bfloat16)
        return carry

    lax.fori_loop(0, chunks, collect, 0)

    def drain(back, carry):
        mine = rank - back * LANES
        far = across - back * LANES

        @pl.when(plane < planes - 1)
        def _():
            block_copy(mine, 0, rank + LANES).wait_send()

        block_copy(mine, 2, across).wait_send()
        block_copy(mine, 1, sibling).wait_send()
        block_copy(far, 1, sibling).wait_send()
        return carry

    lax.fori_loop(0, plane + 1, drain, 0)

    def drain_sums(chunk, carry):
        for step in range(1, tp_count):
            sum_copy(lax.rem(tp_rank + step, tp_count), tp_rank, chunk).wait_send()
        return carry

    lax.fori_loop(0, chunks, drain_sums, 0)


def body(ctx_count, tp_count, queries, keys, values, head_kind, sink_len, window_len, w_out):
    rows, q_cols = queries.shape
    kv_cols = keys.shape[1]
    heads = q_cols // HD
    in_cols, out_cols = w_out.shape
    share = rows // tp_count
    chunks = out_cols // CHUNK
    vmem = pl.BlockSpec(memory_space=pltpu.VMEM)
    smem = pl.BlockSpec(memory_space=pltpu.SMEM)
    return pl.pallas_call(
        functools.partial(layer_kernel, ctx_count, tp_count),
        out_shape=jax.ShapeDtypeStruct((share, out_cols), jnp.bfloat16),
        in_specs=[smem, smem, smem, vmem, vmem, vmem, pl.BlockSpec(memory_space=pl.ANY)],
        out_specs=vmem,
        scratch_shapes=[
            pltpu.VMEM((ctx_count * rows, 2 * kv_cols), jnp.bfloat16),
            pltpu.VMEM((in_cols, out_cols), jnp.bfloat16),
            pltpu.VMEM((heads, rows, HD), jnp.float32),
            pltpu.VMEM((heads, rows, 2 * HD), jnp.float32),
            pltpu.VMEM((rows, 2 * rows), jnp.float32),
            pltpu.VMEM((rows, q_cols), jnp.bfloat16),
            pltpu.VMEM((rows, CHUNK), jnp.float32),
            pltpu.VMEM((rows, out_cols), jnp.bfloat16),
            pltpu.VMEM((rows, out_cols), jnp.bfloat16),
            pltpu.VMEM((share, out_cols), jnp.float32),
            pltpu.SemaphoreType.DMA,
            pltpu.SemaphoreType.DMA((ctx_count, 3)),
            pltpu.SemaphoreType.DMA((ctx_count,)),
            pltpu.SemaphoreType.DMA((tp_count, chunks)),
            pltpu.SemaphoreType.DMA((tp_count, chunks)),
        ],
        compiler_params=pltpu.CompilerParams(
            collective_id=0, has_side_effects=True, vmem_limit_bytes=56 * 2**20
        ),
    )(head_kind, sink_len, window_len, queries, keys, values, w_out)


def solution(mesh):
    in_specs = (P("ctx", "tp"), P("ctx", "tp"), P("ctx", "tp"), P(), P(), P(), P("tp", None))
    out_specs = P(("ctx", "tp"), None)
    run = functools.partial(body, mesh.shape["ctx"], mesh.shape["tp"])
    return jax.shard_map(run, mesh=mesh, in_specs=in_specs, out_specs=out_specs, check_vma=False)
```

```python
import functools
import math

import jax
import jax.numpy as jnp
from jax import lax
from jax.experimental import pallas as pl
from jax.experimental.pallas import tpu as pltpu
from jax.sharding import PartitionSpec as P

HD = 128
LANES = 4
CHUNK = 512
LOW = -1e30
MESH = pl.DeviceIdType.MESH


def layer_kernel(
    ctx_count, tp_count, kind_ref, sink_ref, window_ref, q_ref, k_ref, v_ref, w_hbm, out_ref,
    kv_buf, w_buf, top_ref, acc_ref, bias_ref, attn_ref, part_ref, send_buf, recv_buf, own_ref,
    w_sem, block_send, block_recv, sum_send, sum_recv,
):
    rank = lax.axis_index("ctx")
    tp_rank = lax.axis_index("tp")
    rows, kv_cols = k_ref.shape
    local_kv = kv_cols // HD
    group = q_ref.shape[1] // kv_cols
    planes = ctx_count // LANES
    plane = lax.div(rank, LANES)
    lane = lax.rem(rank, LANES)
    odd = lax.rem(lane, 2)
    high = lax.div(lane, 2)
    sibling = rank + 1 - 2 * odd
    across = rank + 2 - 4 * high
    factor = math.log2(math.e) / math.sqrt(HD)
    out_cols = w_buf.shape[1]
    chunks = out_cols // CHUNK
    share = rows // tp_count

    barrier = pltpu.get_barrier_semaphore()

    def greet(where):
        pl.semaphore_signal(barrier, inc=1, device_id=where, device_id_type=MESH)

    greet({"ctx": sibling})
    greet({"ctx": across})
    for step in range(1, tp_count):
        greet({"tp": lax.rem(tp_rank + step, tp_count)})

    @pl.when(plane > 0)
    def _():
        greet({"ctx": rank - LANES})

    @pl.when(plane < planes - 1)
    def _():
        greet({"ctx": rank + LANES})

    own_rows = pl.ds(pl.multiple_of(rank * rows, rows), rows)
    kv_buf[own_rows, :kv_cols] = k_ref[...]
    kv_buf[own_rows, kv_cols:] = v_ref[...]

    beside_planes = jnp.minimum(plane, 1) + jnp.minimum(planes - 1 - plane, 1)
    pl.semaphore_wait(barrier, 1 + tp_count + beside_planes)

    def block_copy(block, way, target):
        where = pl.ds(pl.multiple_of(block * rows, rows), rows)
        return pltpu.make_async_remote_copy(
            src_ref=kv_buf.at[where],
            dst_ref=kv_buf.at[where],
            send_sem=block_send.at[block, way],
            recv_sem=block_recv.at[block],
            device_id={"ctx": target},
            device_id_type=MESH,
        )

    def send_on(block):
        @pl.when(plane < planes - 1)
        def _():
            block_copy(block, 0, rank + LANES).start()

        block_copy(block, 2, across).start()
        block_copy(block, 1, sibling).start()

    def fold(first_block):
        span = 2 * rows
        key_rows = pl.ds(pl.multiple_of(first_block * rows, rows), span)
        parts = span // HD

        def head_step(head, carry):
            index = tp_rank * local_kv + head
            reach = jnp.where(kind_ref[index] == 1, jnp.int32(2**30), window_ref[index])
            key_pos = first_block * rows + lax.broadcasted_iota(jnp.int32, (rows, span), 1)
            behind = key_pos - rank * rows - lax.broadcasted_iota(jnp.int32, (rows, span), 0)
            allowed = (behind <= 0) & ((behind > -reach) | (key_pos < sink_ref[index]))
            bias_ref[...] = jnp.where(allowed, 0.0, LOW)
            key_block = kv_buf[key_rows, pl.ds(pl.multiple_of(head * HD, HD), HD)]
            value_block = kv_buf[key_rows, pl.ds(pl.multiple_of(kv_cols + head * HD, HD), HD)]
            value_block = jnp.concatenate([value_block, jnp.ones_like(value_block)], axis=1)
            for member in range(group):
                slot = head * group + member
                query = q_ref[:, pl.ds(pl.multiple_of(slot * HD, HD), HD)]
                scores = lax.dot_general(
                    query, key_block, (((1,), (1,)), ((), ())),
                    preferred_element_type=jnp.float32,
                )
                scores = scores * factor + bias_ref[...]
                before = top_ref[slot]
                top = jnp.maximum(before, jnp.max(scores, axis=1, keepdims=True))
                weights = jnp.concatenate(
                    [
                        jnp.exp2(scores[:, i * HD : (i + 1) * HD] - top).astype(jnp.bfloat16)
                        for i in range(parts)
                    ],
                    axis=1,
                )
                keep = jnp.exp2(before - top)
                blended = jnp.dot(weights, value_block, preferred_element_type=jnp.float32)
                top_ref[slot] = top
                acc_ref[slot, :, :HD] = acc_ref[slot, :, :HD] * keep + blended[:, :HD]
                acc_ref[slot, :, HD:] = acc_ref[slot, :, HD:] * keep + blended[:, HD:]
            return carry

        lax.fori_loop(0, local_kv, head_step, 0)

    send_on(rank)
    w_copy = pltpu.make_async_copy(w_hbm, w_buf, w_sem)
    w_copy.start()
    top_ref[...] = jnp.full_like(top_ref, LOW)
    acc_ref[...] = jnp.zeros_like(acc_ref)

    def plane_step(back, carry):
        mine = rank - back * LANES
        beside = sibling - back * LANES
        far = across - back * LANES
        far_beside = far + 1 - 2 * odd
        near_pair = mine - odd
        far_pair = far - odd

        @pl.when(back < plane)
        def _():
            block_copy(mine - LANES, 0, rank).wait_recv()
            send_on(mine - LANES)

        block_copy(beside, 0, rank).wait_recv()
        fold(near_pair)
        block_copy(far, 0, rank).wait_recv()
        block_copy(far, 1, sibling).start()
        block_copy(far_beside, 0, rank).wait_recv()

        @pl.when(far_pair <= rank)
        def _():
            fold(far_pair)

        return carry

    lax.fori_loop(0, plane + 1, plane_step, 0)

    for slot in range(local_kv * group):
        attn_ref[:, slot * HD : (slot + 1) * HD] = (
            acc_ref[slot, :, :HD] / acc_ref[slot, :, HD:]
        ).astype(jnp.bfloat16)
    w_copy.wait()

    def sum_copy(target, source, chunk):
        where = pl.ds(pl.multiple_of(chunk * CHUNK, CHUNK), CHUNK)
        return pltpu.make_async_remote_copy(
            src_ref=send_buf.at[pl.ds(pl.multiple_of(target * share, share), share), where],
            dst_ref=recv_buf.at[pl.ds(pl.multiple_of(source * share, share), share), where],
            send_sem=sum_send.at[target, chunk],
            recv_sem=sum_recv.at[source, chunk],
            device_id={"tp": target},
            device_id_type=MESH,
        )

    def project(chunk, carry):
        where = pl.ds(pl.multiple_of(chunk * CHUNK, CHUNK), CHUNK)
        part_ref[...] = jnp.dot(attn_ref[...], w_buf[:, where], preferred_element_type=jnp.float32)
        send_buf[:, where] = part_ref[...].astype(jnp.bfloat16)
        for step in range(1, tp_count):
            sum_copy(lax.rem(tp_rank + step, tp_count), tp_rank, chunk).start()
        own_ref[:, where] = part_ref[pl.ds(pl.multiple_of(tp_rank * share, share), share), :]
        return carry

    lax.fori_loop(0, chunks, project, 0)

    def collect(chunk, carry):
        where = pl.ds(pl.multiple_of(chunk * CHUNK, CHUNK), CHUNK)
        total = own_ref[:, where]
        for step in range(1, tp_count):
            source = lax.rem(tp_rank + step, tp_count)
            sum_copy(source, source, chunk).wait_recv()
            rows_from = pl.ds(pl.multiple_of(source * share, share), share)
            total = total + recv_buf[rows_from, where].astype(jnp.float32)
        out_ref[:, where] = total.astype(jnp.bfloat16)
        return carry

    lax.fori_loop(0, chunks, collect, 0)

    def drain(back, carry):
        mine = rank - back * LANES
        far = across - back * LANES

        @pl.when(plane < planes - 1)
        def _():
            block_copy(mine, 0, rank + LANES).wait_send()

        block_copy(mine, 2, across).wait_send()
        block_copy(mine, 1, sibling).wait_send()
        block_copy(far, 1, sibling).wait_send()
        return carry

    lax.fori_loop(0, plane + 1, drain, 0)

    def drain_sums(chunk, carry):
        for step in range(1, tp_count):
            sum_copy(lax.rem(tp_rank + step, tp_count), tp_rank, chunk).wait_send()
        return carry

    lax.fori_loop(0, chunks, drain_sums, 0)


def body(ctx_count, tp_count, queries, keys, values, head_kind, sink_len, window_len, w_out):
    rows, q_cols = queries.shape
    kv_cols = keys.shape[1]
    heads = q_cols // HD
    in_cols, out_cols = w_out.shape
    share = rows // tp_count
    chunks = out_cols // CHUNK
    vmem = pl.BlockSpec(memory_space=pltpu.VMEM)
    smem = pl.BlockSpec(memory_space=pltpu.SMEM)
    return pl.pallas_call(
        functools.partial(layer_kernel, ctx_count, tp_count),
        out_shape=jax.ShapeDtypeStruct((share, out_cols), jnp.bfloat16),
        in_specs=[smem, smem, smem, vmem, vmem, vmem, pl.BlockSpec(memory_space=pl.ANY)],
        out_specs=vmem,
        scratch_shapes=[
            pltpu.VMEM((ctx_count * rows, 2 * kv_cols), jnp.bfloat16),
            pltpu.VMEM((in_cols, out_cols), jnp.bfloat16),
            pltpu.VMEM((heads, rows, HD), jnp.float32),
            pltpu.VMEM((heads, rows, 2 * HD), jnp.float32),
            pltpu.VMEM((rows, 2 * rows), jnp.float32),
            pltpu.VMEM((rows, q_cols), jnp.bfloat16),
            pltpu.VMEM((rows, CHUNK), jnp.float32),
            pltpu.VMEM((rows, out_cols), jnp.bfloat16),
            pltpu.VMEM((rows, out_cols), jnp.bfloat16),
            pltpu.VMEM((share, out_cols), jnp.float32),
            pltpu.SemaphoreType.DMA,
            pltpu.SemaphoreType.DMA((ctx_count, 3)),
            pltpu.SemaphoreType.DMA((ctx_count,)),
            pltpu.SemaphoreType.DMA((tp_count, chunks)),
            pltpu.SemaphoreType.DMA((tp_count, chunks)),
        ],
        compiler_params=pltpu.CompilerParams(
            collective_id=0, has_side_effects=True, vmem_limit_bytes=56 * 2**20
        ),
    )(head_kind, sink_len, window_len, queries, keys, values, w_out)


def solution(mesh):
    in_specs = (P("ctx", "tp"), P("ctx", "tp"), P("ctx", "tp"), P(), P(), P(), P("tp", None))
    out_specs = P(("ctx", "tp"), None)
    run = functools.partial(body, mesh.shape["ctx"], mesh.shape["tp"])
    return jax.shard_map(run, mesh=mesh, in_specs=in_specs, out_specs=out_specs, check_vma=False)
```
